256 devices in a mesh: dp: 16 (over z_hi, x, core), tensor: 16 (over z_lo, y).
Axes of the slice: x: 4, y: 4, z: 8 (z_hi: 2, z_lo: 4; z = z_hi * 4 + z_lo), core: 2. Of those that a mesh axis runs over, the one named last changes fastest.
Arguments:
- train_hidden: bfloat16 [48, 256, 28672], P('dp', None, 'tensor'), may hold values from -6 to 6
- train_grad: bfloat16 [48, 256, 8192], P('dp', None, 'tensor'), may hold values from -6 to 6
- val_hidden: bfloat16 [16, 128, 28672], P('dp', None, 'tensor'), may hold values from -6 to 6
- val_grad: bfloat16 [16, 128, 8192], P('dp', None, 'tensor'), may hold values from -6 to 6
- train_lengths: int32 [48], P('dp'), may hold values from 1 to 256, as said below
- train_buckets: int32 [48], P('dp'), may hold values from 0 to 3, as said below
- val_lengths: int32 [16], replicated, may hold values from 1 to 128, as said below
- bucket_weight: float32 [4], replicated, may hold values from 0.5 to 2
Outputs:
- scores: float32 [48, 16], P('dp')
The draws below stay inside these ranges and needn't reach their ends.
Inputs may be any that keep to these rules, and one draw needn't show every extreme that they name: `train_lengths`: bucket b holds lengths from b * 64 + 1 to (b + 1) * 64; some prompt of bucket 3 has exactly 256 tokens. `train_buckets`: both the first and the last bucket occur. `val_lengths`: some validation prompt has exactly 128 tokens.
All inputs are finite; a program needn't handle non-finite values.
Results may differ from the reference program's by a relative error of at most 0.0003.
Values may be sent and summed in bfloat16 or wider, within the bound.
A program may use at most 128 MiB of HBM per device.

```python
import math
import jax
import jax.numpy as jnp
from jax import lax

D = 8192
FF = 28672
L = 256
LV = 128
NBUCKET = 4
NTRAIN = 48
NVAL = 16


def train_profile(key):
    key_bucket, key_length, key_pick = jax.random.split(key, 3)
    buckets = jax.random.randint(key_bucket, (NTRAIN,), 0, NBUCKET)
    pick = jax.random.randint(key_pick, (), 0, NTRAIN)
    places = jnp.arange(NTRAIN)
    buckets = jnp.where(places == pick, NBUCKET - 1, buckets)
    buckets = jnp.where(places == (pick + 1) % NTRAIN, 0, buckets)
    width_each = L // NBUCKET
    lengths = buckets * width_each + 1 + jax.random.randint(key_length, (NTRAIN,), 0, width_each)
    lengths = jnp.where(places == pick, L, lengths)
    return (buckets.astype(jnp.int32), lengths.astype(jnp.int32))


def draw_train_lengths(key, part):
    shared = train_profile(key)
    return shared[1]


def draw_train_buckets(key, part):
    shared = train_profile(key)
    return shared[0]


def draw_val_lengths(key, part):
    key = jax.random.fold_in(key, 5)
    key_length, key_pick = jax.random.split(key)
    lengths = jax.random.randint(key_length, (NVAL,), 1, LV + 1)
    pick = jax.random.randint(key_pick, (), 0, NVAL)
    lengths = jnp.where(jnp.arange(NVAL) == pick, LV, lengths)
    return lengths.astype(jnp.int32)


def shard_levels(rng, shape, shards, least, largest):
    gain = 1.0
    for dim, blocks in shards:
        heights = jax.random.uniform(jax.random.fold_in(jax.random.fold_in(rng, 6), dim), (blocks,), jnp.float32, least / len(shards), largest / len(shards))
        gain = gain * jnp.repeat(jnp.exp(heights), shape[dim] // blocks).reshape((-1,) + (1,) * (len(shape) - 1 - dim))
    return gain


def normal_values(own_key, shape, width, reach, cuts=(), held_as=jnp.bfloat16):
    gain = shard_levels(own_key, shape, cuts, -0.22, 0.18) if cuts else 1.0
    values = jax.random.normal(own_key, shape, jnp.float32) * width * gain
    return jnp.minimum(jnp.maximum(values, -reach), reach).astype(held_as)


def setup_inputs(seed: int = 0) -> dict:
    keys = jax.random.split(jax.random.key(seed), 9)
    train_hidden = normal_values(keys[0], (NTRAIN, L, FF), 1.0, 6.0, ((0, 16), (2, 16)))
    train_grad = normal_values(keys[1], (NTRAIN, L, D), 1.0, 6.0, ((0, 16), (2, 16)))
    val_hidden = normal_values(keys[2], (NVAL, LV, FF), 1.0, 6.0, ((0, 16), (2, 16)))
    val_grad = normal_values(keys[3], (NVAL, LV, D), 1.0, 6.0, ((0, 16), (2, 16)))
    train_lengths = draw_train_lengths(jax.random.fold_in(keys[8], 71), 0)
    train_buckets = draw_train_buckets(jax.random.fold_in(keys[8], 71), 0)
    val_lengths = draw_val_lengths(jax.random.fold_in(keys[8], 71), 0)
    bucket_weight = jnp.clip(jnp.exp(jax.random.uniform(keys[7], (NBUCKET,), jnp.float32, math.log(0.5), math.log(2.0))), 0.5, 2.0)
    return dict(train_hidden=train_hidden, train_grad=train_grad, val_hidden=val_hidden, val_grad=val_grad, train_lengths=train_lengths, train_buckets=train_buckets, val_lengths=val_lengths, bucket_weight=bucket_weight)


def reference(train_hidden, train_grad, val_hidden, val_grad, train_lengths, train_buckets, val_lengths, bucket_weight):
    train_mask = jnp.arange(L)[None, :] < train_lengths[:, None]
    train_masked = jnp.where(train_mask[:, :, None], train_hidden, jnp.zeros((), jnp.bfloat16))
    val_mask = jnp.arange(LV)[None, :] < val_lengths[:, None]
    val_masked = jnp.where(val_mask[:, :, None], val_hidden, jnp.zeros((), jnp.bfloat16))
    val_flat = val_masked.reshape(NVAL * LV, FF)
    grad_flat = val_grad.reshape(NVAL * LV, D)

    def one_prompt(pair):
        hidden_rows, grad_rows = pair
        hidden_gram = lax.dot_general(hidden_rows, val_flat, (((1,), (1,)), ((), ())), preferred_element_type=jnp.float32)
        grad_gram = lax.dot_general(grad_rows, grad_flat, (((1,), (1,)), ((), ())), preferred_element_type=jnp.float32)
        return lax.optimization_barrier(jnp.sum((hidden_gram * grad_gram).reshape(L, NVAL, LV), axis=(0, 2)))
    pair_sum = lax.map(one_prompt, (train_masked, train_grad))
    chosen = (train_buckets[:, None] == jnp.arange(NBUCKET)[None, :]).astype(jnp.float32)
    weight = lax.optimization_barrier(jnp.sum(chosen * bucket_weight[None, :], axis=1))
    counts = train_lengths.astype(jnp.float32)[:, None] * val_lengths.astype(jnp.float32)[None, :]
    return pair_sum * weight[:, None] / (math.sqrt(FF * D) * jnp.sqrt(counts))
```

```python
import functools
import math

import jax
import jax.numpy as jnp
from jax import lax
from jax.experimental import pallas as pl
from jax.experimental.pallas import tpu as pltpu
from jax.sharding import PartitionSpec as P

MESH = pl.DeviceIdType.MESH
D = 8192
FF = 28672
TOP = 32000.0
STEPS = 8.0
ROWS = 1536
HALF = 768
PIECE = 96
CODE = 16
SLOT = PIECE + CODE
RS_ROWS = (768, 384, 192, 96)
ORDER = (0, 1, 3, 2, 4, 5, 7, 6)


def quantize(x):
    top = jnp.maximum(jnp.max(jnp.abs(x), axis=0, keepdims=True), 1e-30)
    code = jnp.ceil(jnp.log2(top) * STEPS)
    q = jnp.round(x * (jnp.exp2(code * (-1.0 / STEPS)) * TOP)).astype(jnp.int32).astype(jnp.int16)
    return q, jnp.broadcast_to(code, (CODE, x.shape[1])).astype(jnp.int32).astype(jnp.int16)


def step_of(code):
    code = code.astype(jnp.int32).astype(jnp.float32)
    return jnp.exp2(code[:1] * (1.0 / STEPS)) * (1.0 / TOP)


def widen(q):
    return q.astype(jnp.int32).astype(jnp.float32)


def kernel(
    tl,
    tb,
    vl,
    bw,
    th,
    tg,
    vh,
    vg,
    out,
    th_b,
    tg_b,
    vh_b,
    vg_b,
    gram,
    hid,
    sb1,
    sb2,
    sb3,
    sb4,
    rb1,
    rb2,
    rb3,
    rb4,
    g_all,
    info,
    total,
    fin1,
    fin2,
    ssem,
    rsem,
    lsem,
):
    dp, tn = lax.axis_index("dp"), lax.axis_index("tensor")
    zh, x, c = dp // 8, (dp // 2) % 4, dp % 2
    zl, y = tn // 4, tn % 4

    def dev(zh=zh, x=x, c=c, zl=zl, y=y):
        return (zh * 8 + x * 2 + c, zl * 4 + y)

    sib = dev(c=1 - c)
    zhp = dev(zh=1 - zh)
    xp, xm, x2 = dev(x=(x + 1) % 4), dev(x=(x + 3) % 4), dev(x=(x + 2) % 4)
    y1, y3 = dev(y=y + 1 - 2 * (y % 2)), dev(y=3 - y)
    z1, z2 = dev(zl=zl + 1 - 2 * (zl % 2)), dev(zl=(zl + 2) % 4)
    fin_y = [
        dev(c=(c + dc) % 2, y=(y + dy) % 4) for dc in range(2) for dy in range(4) if dc + dy > 0
    ]
    fin_z = [dev(zl=(zl + dz) % 4) for dz in range(1, 4)]
    g0, g1 = (y % 2 + y // 2) % 2, y // 2
    z0, zb = zl % 2, zl // 2

    pending = []
    count = [0]

    def send(src, dst, to):
        i = count[0]
        count[0] += 1
        copy = pltpu.make_async_remote_copy(
            src_ref=src,
            dst_ref=dst,
            send_sem=ssem.at[i],
            recv_sem=rsem.at[i],
            device_id=to,
            device_id_type=MESH,
        )
        copy.start()
        pending.append(copy)
        return copy

    own = [
        pltpu.make_async_copy(vg, vg_b.at[pl.ds(0, 128)], lsem.at[0]),
        pltpu.make_async_copy(tg, tg_b.at[pl.ds(0, HALF)], lsem.at[1]),
        pltpu.make_async_copy(vh, vh_b.at[pl.ds(0, 128)], lsem.at[2]),
        pltpu.make_async_copy(th, th_b.at[pl.ds(0, HALF)], lsem.at[3]),
    ]
    for copy in own:
        copy.start()
    row8 = lax.broadcasted_iota(jnp.int32, (8, 128), 0)
    lane8 = lax.broadcasted_iota(jnp.int32, (8, 128), 1)
    info[0] = jnp.where(row8 == 0, tl[0], jnp.where(row8 == 1, tl[1], tl[2])).astype(jnp.float32)

    barrier = pltpu.get_barrier_semaphore()
    peers = [zhp, xp, xm, x2, z1, z2, fin_z[2]] + fin_y
    peers = [zhp, xp, xm, x2] + fin_z + fin_y
    for peer in peers:
        pl.semaphore_signal(barrier, inc=1, device_id=peer, device_id_type=MESH)
    pl.semaphore_wait(barrier, len(peers))

    def vslot(ref, s, half=None):
        return ref.at[pl.ds(128 * s, 128)] if half is None else ref.at[pl.ds(128 * s + 64 * half, 64)]

    arrived = {}
    arrived["g4"] = send(vg, vslot(vg_b, 4), zhp)
    arrived["g1"] = send(vg, vslot(vg_b, 1), xp)
    arrived["g3"] = send(vg, vslot(vg_b, 3), xm)
    arrived["g2"] = send(vg, vslot(vg_b, 2), x2)
    arrived["tg"] = send(tg, tg_b.at[pl.ds(HALF, HALF)], sib)
    arrived["info"] = send(info.at[0], info.at[1], sib)

    def vh_half(h):
        return vh.at[pl.ds(64 * h, 64)]

    ops = []

    def at(time, fn):
        ops.append((time, len(ops), fn))

    def start_hidden():
        arrived["h4", 0] = send(vh_half(0), vslot(vh_b, 4, 0), zhp)
        arrived["h1", 0] = send(vh_half(0), vslot(vh_b, 1, 0), xp)
        arrived["h3", 1] = send(vh_half(1), vslot(vh_b, 3, 1), xm)
        arrived["th"] = send(th, th_b.at[pl.ds(HALF, HALF)], sib)
        arrived["h1", 1] = send(vh_half(1), vslot(vh_b, 1, 1), xp)
        arrived["h3", 0] = send(vh_half(0), vslot(vh_b, 3, 0), xm)
        arrived["h4", 1] = send(vh_half(1), vslot(vh_b, 4, 1), zhp)

    at(3.0, start_hidden)

    def forward_own():
        arrived["h1", 0].wait_recv()
        arrived["h2", 0] = send(vslot(vh_b, 1, 0), vslot(vh_b, 2, 0), xp)
        arrived["h3", 1].wait_recv()
        arrived["h2", 1] = send(vslot(vh_b, 3, 1), vslot(vh_b, 2, 1), xm)

    at(16.0, forward_own)

    def forward_far(h):
        arrived["h4", h].wait_recv()
        arrived["h5", h] = send(vslot(vh_b, 4, h), vslot(vh_b, 5, h), xp)
        arrived["h7", h] = send(vslot(vh_b, 4, h), vslot(vh_b, 7, h), xm)

    at(21.0, lambda: forward_far(0))
    at(29.0, lambda: forward_far(1))

    def forward_last():
        arrived["h5", 0].wait_recv()
        arrived["h6", 0] = send(vslot(vh_b, 5, 0), vslot(vh_b, 6, 0), xp)
        arrived["h7", 1].wait_recv()
        arrived["h6", 1] = send(vslot(vh_b, 7, 1), vslot(vh_b, 6, 1), xm)

    at(38.0, forward_last)

    def forward_grad():
        arrived["g4"].wait_recv()
        arrived["g5"] = send(vslot(vg_b, 4), vslot(vg_b, 5), xp)
        arrived["g7"] = send(vslot(vg_b, 4), vslot(vg_b, 7), xm)
        arrived["g6"] = send(vslot(vg_b, 4), vslot(vg_b, 6), x2)

    at(10.5, forward_grad)

    def mask_train():
        own[1].wait()
        arrived["info"].wait_recv()
        arrived["tg"].wait_recv()
        token = lax.broadcasted_iota(jnp.int32, (256, 128), 0).astype(jnp.float32)
        for i in range(6):
            keep = token < info[i // 3, i % 3 : i % 3 + 1, :]
            rows = pl.ds(256 * i, 256)
            for j in range(4):
                cols = pl.ds(128 * j, 128)
                tg_b[rows, cols] = jnp.where(
                    keep, tg_b[rows, cols].astype(jnp.float32), 0.0
                ).astype(jnp.bfloat16)

    at(5.0, mask_train)

    contract = (((1,), (1,)), ((), ()))
    sbs, rbs = (sb1, sb2, sb3, sb4), (rb1, rb2, rb3, rb4)

    def way(k):
        if k % 2 == 0:
            return ((g0, y1), (g1, y3), (z0, z1), (zb, z2))
        return ((g1, y3), (g0, y1), (z0, z1), (zb, z2))

    def send_part(k, step, x):
        n = RS_ROWS[step]
        q, code = quantize(x)
        sbs[step][k, pl.ds(0, n), :] = q
        sbs[step][k, pl.ds(n, CODE), :] = code
        arrived["r", k, step] = send(sbs[step].at[k], rbs[step].at[k], way(k)[step][1])

    base = {}

    def begin(k):
        s = ORDER[k]
        if s == 0:
            own[0].wait()
        elif s != 4:
            arrived["g%d" % s].wait_recv()
        rhs = vg_b[pl.ds(128 * s, 128), :]

        @pl.loop(0, ROWS // 256)
        def _(i):
            rows = pl.ds(pl.multiple_of(i * 256, 256), 256)
            gram[k, rows, :] = lax.dot_general(
                tg_b[rows, :], rhs, contract, preferred_element_type=jnp.float32
            )

        bit = way(k)[0][0]
        base[k] = bit * 768
        send_part(k, 0, gram[k, pl.ds(pl.multiple_of((1 - bit) * 768, 768), 768), :])

    def middle(k, step):
        arrived["r", k, step - 1].wait_recv()
        n = RS_ROWS[step]
        bit = way(k)[step][0]
        got = rbs[step - 1]
        scale = step_of(got[k, pl.ds(2 * n, CODE), :])

        def summed(part):
            there = pl.ds(pl.multiple_of(base[k] + part * n, 96), n)
            here = pl.ds(pl.multiple_of(part * n, 96), n)
            return there, gram[k, there, :] + widen(got[k, here, :]) * scale

        send_part(k, step, summed(1 - bit)[1])
        there, kept = summed(bit)
        gram[k, there, :] = kept
        base[k] = base[k] + bit * n

    place = {}

    def ready(k):
        arrived["r", k, 3].wait_recv()
        scale = step_of(rb4[k, pl.ds(PIECE, CODE), :])
        there = pl.ds(pl.multiple_of(base[k], 96), PIECE)
        q, code = quantize(gram[k, there, :] + widen(rb4[k, pl.ds(0, PIECE), :]) * scale)
        b = [bit for bit, _ in way(k)]
        spots = [0]
        for i, bit in enumerate(b):
            spots.append(spots[-1] + bit * (8 >> i))
        place[k] = spots
        spot = pl.multiple_of(spots[4] * SLOT, CODE)
        g_all[k, pl.ds(spot, PIECE), :] = q
        g_all[k, pl.ds(pl.multiple_of(spot + PIECE, CODE), CODE), :] = code
        give(k, 3)

    def give(k, step):
        block = g_all.at[
            k, pl.ds(pl.multiple_of(place[k][step + 1] * SLOT, CODE), (8 >> step) * SLOT)
        ]
        arrived["a", k, step] = send(block, block, way(k)[step][1])

    def pass_on(k, step):
        arrived["a", k, step + 1].wait_recv()
        give(k, step)

    def times(k):
        pair = k // 2
        t0 = (6.0, 8.0, 9.0, 13.0, 20.0, 20.5, 26.0, 26.5)[k]
        return [t0, t0 + 7, t0 + 12, t0 + 16, t0 + 20, t0 + 23, t0 + 27, t0 + 32]

    for k in range(8):
        t = times(k)
        at(t[0], functools.partial(begin, k))
        for step in (1, 2, 3):
            at(t[step], functools.partial(middle, k, step))
        at(t[4], functools.partial(ready, k))
        for i, step in enumerate((2, 1, 0)):
            at(t[5 + i], functools.partial(pass_on, k, step))

    def hidden(k):
        s = ORDER[k]
        if k == 0:
            own[2].wait()
            own[3].wait()
            arrived["th"].wait_recv()
        for h in range(2):
            key = ("h%d" % s, h)
            if s != 0 and key not in waited:
                arrived[key].wait_recv()
        rhs = vh_b[pl.ds(128 * s, 128), :]

        @pl.loop(0, ROWS // 256)
        def _(i):
            rows = pl.ds(pl.multiple_of(i * 256, 256), 256)
            hid[k, rows, :] = lax.dot_general(
                th_b[rows, :], rhs, contract, preferred_element_type=jnp.float32
            )

    waited = {("h1", 0), ("h3", 1), ("h4", 0), ("h4", 1), ("h5", 0), ("h7", 1)}
    for k, t in enumerate((14.5, 22.0, 22.2, 27.0, 32.0, 44.0, 44.2, 46.0)):
        at(t, functools.partial(hidden, k))

    total[...] = jnp.zeros_like(total)

    def product(k):
        arrived["a", k, 0].wait_recv()
        s = ORDER[k]
        sums = [None] * 6
        for p in range(16):
            scale = step_of(g_all[k, pl.ds(p * SLOT + PIECE, CODE), :])
            both = hid[k, pl.ds(p * PIECE, PIECE), :] * widen(g_all[k, pl.ds(p * SLOT, PIECE), :])
            parts = {}
            for u in range(6):
                i = (p * 6 + u) // 16
                part = both[16 * u : 16 * u + 8] + both[16 * u + 8 : 16 * u + 16]
                parts[i] = part if i not in parts else parts[i] + part
            for i, part in parts.items():
                part = part * scale
                sums[i] = part if sums[i] is None else sums[i] + part
        tile = jnp.zeros((8, 128), jnp.float32)
        for i in range(6):
            tile = jnp.where(row8 == i, jnp.sum(sums[i], axis=0, keepdims=True), tile)
        far, r = s // 4, s % 4
        prompt = ((zh + far) % 2) * 8 + ((x + 4 - r) % 4) * 2 + c
        tile = jnp.where(lane8 < vl[prompt], tile, 0.0)
        total[...] += jnp.where(lane8 == prompt, jnp.sum(tile, axis=1, keepdims=True), 0.0)

    for k in range(8):
        at(max(times(k)[7] + 7, 46.5), functools.partial(product, k))

    for _, _, fn in sorted(ops, key=lambda op: op[:2]):
        fn()

    mine = total[...]
    turned = jnp.where(row8 < 3, pltpu.roll(mine, 5, 0), pltpu.roll(mine, 3, 0))
    fin1[0] = jnp.where(c == 0, mine, turned)
    last = [send(fin1.at[0], fin1.at[1 + i], peer) for i, peer in enumerate(fin_y)]
    for copy in last:
        copy.wait_recv()
    fin2[0] = jnp.sum(fin1[...], axis=0)
    last = [send(fin2.at[0], fin2.at[1 + i], peer) for i, peer in enumerate(fin_z)]
    for copy in last:
        copy.wait_recv()
    pair = jnp.sum(fin2[...], axis=0)
    pair = jnp.where(c == 0, pair, pltpu.roll(pair, 5, 0))
    weight = jnp.where(row8 == 0, bw[tb[0]], jnp.where(row8 == 1, bw[tb[1]], bw[tb[2]]))
    val_counts = jnp.ones((8, 128), jnp.float32)
    for j in range(16):
        val_counts = jnp.where(lane8 == j, vl[j].astype(jnp.float32), val_counts)
    scores = pair * weight / (math.sqrt(FF * D) * jnp.sqrt(info[0] * val_counts))
    out[...] = scores[:3, :16]
    for copy in pending:
        copy.wait_send()


def local(
    train_hidden,
    train_grad,
    val_hidden,
    val_grad,
    train_lengths,
    train_buckets,
    val_lengths,
    bucket_weight,
):
    smem = pl.BlockSpec(memory_space=pltpu.SMEM)
    hbm = pl.BlockSpec(memory_space=pl.ANY)
    n = 8
    i16, f32, bf16 = jnp.int16, jnp.float32, jnp.bfloat16
    copies = 8 * n + 7 + 14 + 3 + 10
    buffers = [pltpu.VMEM((n, r + CODE, 128), i16) for r in RS_ROWS]
    return pl.pallas_call(
        kernel,
        out_shape=jax.ShapeDtypeStruct((3, 16), f32),
        in_specs=[smem] * 4 + [hbm] * 4,
        out_specs=pl.BlockSpec(memory_space=pltpu.VMEM),
        scratch_shapes=[
            pltpu.VMEM((ROWS, 1792), bf16),
            pltpu.VMEM((ROWS, 512), bf16),
            pltpu.VMEM((1024, 1792), bf16),
            pltpu.VMEM((1024, 512), bf16),
            pltpu.VMEM((n, ROWS, 128), f32),
            pltpu.VMEM((n, ROWS, 128), f32),
            *buffers,
            *buffers,
            pltpu.VMEM((n, 16 * SLOT, 128), i16),
            pltpu.VMEM((2, 8, 128), f32),
            pltpu.VMEM((8, 128), f32),
            pltpu.VMEM((8, 8, 128), f32),
            pltpu.VMEM((4, 8, 128), f32),
            pltpu.SemaphoreType.DMA((copies,)),
            pltpu.SemaphoreType.DMA((copies,)),
            pltpu.SemaphoreType.DMA((4,)),
        ],
        compiler_params=pltpu.CompilerParams(
            collective_id=0, has_side_effects=True, vmem_limit_bytes=56 * 2**20
        ),
        name="ghost",
    )(
        train_lengths,
        train_buckets,
        val_lengths,
        bucket_weight,
        train_hidden.reshape(HALF, 1792),
        train_grad.reshape(HALF, 512),
        val_hidden.reshape(128, 1792),
        val_grad.reshape(128, 512),
    )


def solution(mesh):
    placed = (
        P("dp", None, "tensor"),
        P("dp", None, "tensor"),
        P("dp", None, "tensor"),
        P("dp", None, "tensor"),
        P("dp"),
        P("dp"),
        P(),
        P(),
    )
    return jax.shard_map(
        local, mesh=mesh, in_specs=placed, out_specs=P("dp", None), check_vma=False
    )
```

```python
import functools
import math

import jax
import jax.numpy as jnp
from jax import lax
from jax.experimental import pallas as pl
from jax.experimental.pallas import tpu as pltpu
from jax.sharding import PartitionSpec as P

MESH = pl.DeviceIdType.MESH
D = 8192
FF = 28672
TOP = 32000.0
STEPS = 8.0
ROWS = 1536
HALF = 768
PIECE = 96
CODE = 16
SLOT = PIECE + CODE
QUARTER = 384
BLOCK = QUARTER + CODE
UP = 192
TILE_G = 512
TILE_H = 512


def quantize(x):
    top = jnp.maximum(jnp.max(jnp.abs(x), axis=0, keepdims=True), 1e-30)
    code = jnp.ceil(jnp.log2(top) * STEPS)
    q = jnp.round(x * (jnp.exp2(code * (-1.0 / STEPS)) * TOP)).astype(jnp.int32).astype(jnp.int16)
    return q, jnp.broadcast_to(code, (CODE, x.shape[1])).astype(jnp.int32).astype(jnp.int16)


def step_of(code, rows=1):
    code = code.astype(jnp.int32).astype(jnp.float32)
    return jnp.exp2(code[:rows] * (1.0 / STEPS)) * (1.0 / TOP)


def widen(q):
    return q.astype(jnp.int32).astype(jnp.float32)


def kernel(
    n_near,
    n_far,
    tl,
    tb,
    vl,
    bw,
    th,
    tg,
    vh,
    vg,
    out,
    th_b,
    tg_b,
    vh_b,
    vg_b,
    gram,
    hid,
    pick,
    right_g,
    right_h,
    sy,
    ry,
    sz,
    rz,
    az,
    g_all,
    info,
    total,
    fin1,
    fin2,
    ssem,
    rsem,
    lsem,
):
    chunks = n_near + n_far
    dp, tn = lax.axis_index("dp"), lax.axis_index("tensor")
    zh, x, c = dp // 8, (dp // 2) % 4, dp % 2
    zl, y = tn // 4, tn % 4

    def dev(zh=zh, x=x, c=c, zl=zl, y=y):
        return (zh * 8 + x * 2 + c, zl * 4 + y)

    sib = dev(c=1 - c)
    zhp = dev(zh=1 - zh)
    xp, xm, x2 = dev(x=(x + 1) % 4), dev(x=(x + 3) % 4), dev(x=(x + 2) % 4)
    ys = [dev(y=(y + i) % 4) for i in (1, 2, 3)]
    zs = [dev(zl=(zl + i) % 4) for i in (1, 2, 3)]
    fin_y = [
        dev(c=(c + dc) % 2, y=(y + dy) % 4) for dc in range(2) for dy in range(4) if dc + dy > 0
    ]

    pending = []
    count = [0]

    def send(src, dst, to):
        i = count[0]
        count[0] += 1
        copy = pltpu.make_async_remote_copy(
            src_ref=src,
            dst_ref=dst,
            send_sem=ssem.at[i],
            recv_sem=rsem.at[i],
            device_id=to,
            device_id_type=MESH,
        )
        copy.start()
        pending.append(copy)
        return copy

    own = [
        pltpu.make_async_copy(vg, vg_b.at[pl.ds(0, 128)], lsem.at[0]),
        pltpu.make_async_copy(tg, tg_b.at[pl.ds(0, HALF)], lsem.at[1]),
        pltpu.make_async_copy(vh, vh_b.at[pl.ds(0, 128)], lsem.at[2]),
        pltpu.make_async_copy(th, th_b.at[pl.ds(0, HALF)], lsem.at[3]),
    ]
    for copy in own:
        copy.start()
    row8 = lax.broadcasted_iota(jnp.int32, (8, 128), 0)
    lane8 = lax.broadcasted_iota(jnp.int32, (8, 128), 1)
    info[0] = jnp.where(row8 == 0, tl[0], jnp.where(row8 == 1, tl[1], tl[2])).astype(jnp.float32)

    barrier = pltpu.get_barrier_semaphore()
    peers = [zhp, xp, xm, x2] + zs + fin_y
    for peer in peers:
        pl.semaphore_signal(barrier, inc=1, device_id=peer, device_id_type=MESH)
    pl.semaphore_wait(barrier, len(peers))

    def place(ref, s, part=0, parts=1):
        return ref.at[pl.ds(128 * s + 128 // parts * part, 128 // parts)]

    def piece(ref, part, parts):
        return ref.at[pl.ds(128 // parts * part, 128 // parts)]

    arrived = {}
    for h in range(2):
        arrived["g", 4, h] = send(piece(vg, h, 2), place(vg_b, 4, h, 2), zhp)
    arrived["g", 1] = send(vg, place(vg_b, 1), xp)
    arrived["g", 2] = send(vg, place(vg_b, 2), xm)
    arrived["g", 3] = send(vg, place(vg_b, 3), x2)
    arrived["tg"] = send(tg, tg_b.at[pl.ds(HALF, HALF)], sib)
    arrived["info"] = send(info.at[0], info.at[1], sib)

    prompts, lens, begins = [], [], []
    near = 0
    so_far = 0
    for s in range(8):
        r = (0, 1, 3, 2)[s % 4]
        prompt = ((zh + s // 4) % 2) * 8 + ((x + 4 - r) % 4) * 2 + c
        prompts.append(prompt)
        lens.append(vl[prompt])
        begins.append(so_far)
        so_far = so_far + lens[s]
        if s == 3:
            near = so_far
    near_done = jnp.minimum(near, 128 * n_near)
    everything = so_far

    def chunk_range(k):
        if k < n_near:
            return 128 * k, 0, 4
        return everything - 128 * (chunks - k), near_done, 8

    def fill_pick(k):
        start, least, places = chunk_range(k)
        row = lax.broadcasted_iota(jnp.int32, (128, 128), 0)
        col = lax.broadcasted_iota(jnp.int32, (128, 128), 1)
        for s in range(places):
            rank = col + begins[s]
            hit = (rank - start == row) & (col < lens[s]) & (rank >= least)
            pick[k, :, pl.ds(128 * s, 128)] = jnp.where(hit, 1.0, 0.0).astype(jnp.bfloat16)

    def packed(k, ref, places):
        return lax.dot_general(
            pick[k, :, pl.ds(0, 128 * places)],
            ref[pl.ds(0, 128 * places), :],
            (((1,), (0,)), ((), ())),
            preferred_element_type=jnp.float32,
        )

    ops = []

    def at(time, fn):
        ops.append((time, len(ops), fn))

    def start_far():
        for q in range(4):
            arrived["h", 4, q] = send(piece(vh, q, 4), place(vh_b, 4, q, 4), zhp)

    def start_near(h):
        arrived["h", 1, h] = send(piece(vh, h, 2), place(vh_b, 1, h, 2), xp)
        arrived["h", 2, 1 - h] = send(piece(vh, 1 - h, 2), place(vh_b, 2, 1 - h, 2), xm)

    def start_train():
        arrived["th"] = send(th, th_b.at[pl.ds(HALF, HALF)], sib)

    waited = set()

    def have(key):
        if key not in waited:
            waited.add(key)
            arrived[key].wait_recv()

    def forward_near():
        have(("h", 1, 0))
        arrived["h", 3, 0] = send(place(vh_b, 1, 0, 2), place(vh_b, 3, 0, 2), xp)
        have(("h", 2, 1))
        arrived["h", 3, 1] = send(place(vh_b, 2, 1, 2), place(vh_b, 3, 1, 2), xm)

    def forward_far(q):
        have(("h", 4, q))
        arrived["h", 5, q] = send(place(vh_b, 4, q, 4), place(vh_b, 5, q, 4), xp)
        arrived["h", 6, q] = send(place(vh_b, 4, q, 4), place(vh_b, 6, q, 4), xm)

    def forward_last(q):
        s, to = (5, xp) if q % 2 == 0 else (6, xm)
        have(("h", s, q))
        arrived["h", 7, q] = send(place(vh_b, s, q, 4), place(vh_b, 7, q, 4), to)

    def forward_grad(h):
        have(("g", 4, h))
        for s, to in ((5, xp), (6, xm), (7, x2)):
            arrived["g", s, h] = send(place(vg_b, 4, h, 2), place(vg_b, s, h, 2), to)

    def mask_train():
        own[1].wait()
        have("info")
        have("tg")
        token = lax.broadcasted_iota(jnp.int32, (256, 128), 0).astype(jnp.float32)
        for i in range(6):
            keep = token < info[i // 3, i % 3 : i % 3 + 1, :]
            rows = pl.ds(256 * i, 256)
            for j in range(4):
                cols = pl.ds(128 * j, 128)
                tg_b[rows, cols] = jnp.where(
                    keep, tg_b[rows, cols].astype(jnp.float32), 0.0
                ).astype(jnp.bfloat16)

    def multiply(ks, left, ref, places, right, tile, to):
        for j, k in enumerate(ks):
            right[:, pl.ds(128 * j, 128)] = packed(k, ref, places).T.astype(jnp.bfloat16)

        @pl.loop(0, ROWS // tile)
        def _(i):
            rows = pl.ds(pl.multiple_of(i * tile, tile), tile)
            both = jnp.dot(
                left[rows, :],
                right[:, pl.ds(0, 128 * len(ks))],
                preferred_element_type=jnp.float32,
            )
            for j, k in enumerate(ks):
                to[k, rows, :] = both[:, 128 * j : 128 * j + 128]

    def put(ref, index, x):
        n = x.shape[0]
        q, code = quantize(x)
        ref[*index, pl.ds(0, n), :] = q
        ref[*index, pl.ds(n, CODE), :] = code

    def begin(ks):
        places = chunk_range(ks[0])[2]
        if 0 in ks:
            own[0].wait()
        for s in range(1, places):
            for key in (("g", s),) if s < 4 else (("g", s, 0), ("g", s, 1)):
                have(key)
        for k in ks:
            fill_pick(k)
        multiply(ks, tg_b, vg_b, places, right_g, TILE_G, gram)
        for k in ks:
            for i in range(3):
                theirs = pl.multiple_of(((y + 1 + i) % 4) * QUARTER, QUARTER)
                put(sy, (k, i), gram[k, pl.ds(theirs, QUARTER), :])
                arrived["y", k, i] = send(sy.at[k, i], ry.at[k, i], ys[i])

    def middle(k):
        for i in range(3):
            have(("y", k, i))
        scales = [step_of(ry[k, i, pl.ds(QUARTER, CODE), :]) for i in range(3)]

        def summed(part):
            here = pl.ds(pl.multiple_of(part * PIECE, PIECE), PIECE)
            there = pl.ds(pl.multiple_of(y * QUARTER + part * PIECE, PIECE), PIECE)
            value = gram[k, there, :]
            for i in range(3):
                value = value + widen(ry[k, i, here, :]) * scales[i]
            return there, value

        for i in range(3):
            put(sz, (k, i), summed((zl + 1 + i) % 4)[1])
            arrived["z", k, i] = send(sz.at[k, i], rz.at[k, i], zs[i])
        there, value = summed(zl)
        gram[k, there, :] = value

    def ready(k):
        for i in range(3):
            have(("z", k, i))
        there = pl.ds(pl.multiple_of(y * QUARTER + zl * PIECE, PIECE), PIECE)
        value = gram[k, there, :]
        for i in range(3):
            scale = step_of(rz[k, i, pl.ds(PIECE, CODE), :])
            value = value + widen(rz[k, i, pl.ds(0, PIECE), :]) * scale
        put(az, (k, 0), value)
        for i in range(3):
            arrived["az", k, i] = send(az.at[k, 0], az.at[k, 1 + i], zs[i])

    def block(k, i, first=0, rows=BLOCK):
        owner = (y + i) % 4
        return g_all.at[k, pl.ds(pl.multiple_of(owner * BLOCK + first, CODE), rows)]

    def spread(k):
        for i in range(3):
            have(("az", k, i))
        codes = jnp.zeros((CODE, 128), jnp.int32)
        row = lax.broadcasted_iota(jnp.int32, (CODE, 128), 0)
        for i in range(4):
            part = (zl + 4 - i) % 4
            spot = pl.multiple_of(y * BLOCK + part * PIECE, CODE)
            g_all[k, pl.ds(spot, PIECE), :] = az[k, i, pl.ds(0, PIECE), :]
            code = az[k, i, pl.ds(PIECE, CODE), :].astype(jnp.int32)
            codes = jnp.where(row == part, code, codes)
        g_all[k, pl.ds(pl.multiple_of(y * BLOCK + QUARTER, CODE), CODE), :] = codes.astype(jnp.int16)
        arrived["up", k] = send(block(k, 0), block(k, 0), ys[0])
        arrived["down", k] = send(block(k, 0), block(k, 0), ys[2])

    def relay(k):
        have(("up", k))
        rows = block(k, 3, 0, UP)
        arrived["up2", k] = send(rows, rows, ys[0])
        have(("down", k))
        rows = block(k, 1, UP, BLOCK - UP)
        arrived["down2", k] = send(rows, rows, ys[2])

    def hidden(ks):
        near_only, last = ks[-1] < n_near, ks[-1] == chunks - 1
        places = 4 if near_only else 8 if last else 7
        if 0 in ks:
            own[2].wait()
            own[3].wait()
            have("th")
        for s in range(1, places):
            for i in range(2 if s < 4 else 4):
                have(("h", s, i))
        multiply(ks, th_b, vh_b, places, right_h, TILE_H, hid)

    total[...] = jnp.zeros_like(total)

    def product(k):
        have(("up2", k))
        have(("down2", k))
        sums = [None] * 6
        for p in range(16):
            top = p // 4 * BLOCK
            if p % 4 == 0:
                steps = step_of(g_all[k, pl.ds(top + QUARTER, CODE), :], 8)
            scale = steps[p % 4 : p % 4 + 1]
            here = pl.ds(top + p % 4 * PIECE, PIECE)
            both = hid[k, pl.ds(p * PIECE, PIECE), :] * widen(g_all[k, here, :])
            parts = {}
            for u in range(6):
                i = (p * 6 + u) // 16
                part = both[16 * u : 16 * u + 8] + both[16 * u + 8 : 16 * u + 16]
                parts[i] = part if i not in parts else parts[i] + part
            for i, part in parts.items():
                part = part * scale
                sums[i] = part if sums[i] is None else sums[i] + part
        tile = jnp.zeros((8, 128), jnp.float32)
        for i in range(6):
            tile = jnp.where(row8 == i, jnp.sum(sums[i], axis=0, keepdims=True), tile)
        start, least, places = chunk_range(k)
        rank = lane8 + start
        for s in range(places):
            mine = (rank >= begins[s]) & (rank < begins[s] + lens[s]) & (rank >= least)
            total[s] += jnp.where(mine, tile, 0.0)

    do = dict(
        start_far=start_far,
        start_near=start_near,
        start_train=start_train,
        forward_near=forward_near,
        forward_far=forward_far,
        forward_last=forward_last,
        forward_grad=forward_grad,
        mask_train=mask_train,
        begin=begin,
        middle=middle,
        ready=ready,
        spread=spread,
        relay=relay,
        hidden=hidden,
        product=product,
    )
    plan(chunks, n_near, at, do)
    for _, _, fn in sorted(ops, key=lambda op: op[:2]):
        fn()

    mine = jnp.zeros((8, 128), jnp.float32)
    for s in range(8):
        mine = jnp.where(lane8 == prompts[s], jnp.sum(total[s], axis=1, keepdims=True), mine)
    turned = jnp.where(row8 < 3, pltpu.roll(mine, 5, 0), pltpu.roll(mine, 3, 0))
    fin1[0] = jnp.where(c == 0, mine, turned)
    last = [send(fin1.at[0], fin1.at[1 + i], peer) for i, peer in enumerate(fin_y)]
    for copy in last:
        copy.wait_recv()
    fin2[0] = jnp.sum(fin1[...], axis=0)
    last = [send(fin2.at[0], fin2.at[1 + i], peer) for i, peer in enumerate(zs)]
    for copy in last:
        copy.wait_recv()
    pair = jnp.sum(fin2[...], axis=0)
    pair = jnp.where(c == 0, pair, pltpu.roll(pair, 5, 0))
    weight = jnp.where(row8 == 0, bw[tb[0]], jnp.where(row8 == 1, bw[tb[1]], bw[tb[2]]))
    val_counts = jnp.ones((8, 128), jnp.float32)
    for j in range(16):
        val_counts = jnp.where(lane8 == j, vl[j].astype(jnp.float32), val_counts)
    scores = pair * weight / (math.sqrt(FF * D) * jnp.sqrt(info[0] * val_counts))
    out[...] = scores[:3, :16]
    for copy in pending:
        copy.wait_send()


def plan(chunks, n_near, at, do):
    def add(time, name, *args):
        at(time, functools.partial(do[name], *args))

    add(0.0, "start_far")
    add(0.1, "start_train")
    add(0.2, "start_near", 0)
    add(16.0, "mask_train")
    add(19.0, "forward_grad", 0)
    add(21.0, "forward_grad", 1)
    add(21.1, "start_near", 1)
    add(29.0, "forward_near")
    for q in range(4):
        add(31.0 + 4.6 * q, "forward_far", q)
        add(37.0 + 4.6 * q, "forward_last", q)
    add(18.0, "begin", tuple(range(n_near)))
    add(29.0, "begin", tuple(range(n_near, chunks)))
    add(43.0, "hidden", tuple(range(n_near)))
    add(53.0, "hidden", tuple(range(n_near, chunks - 1)))
    add(55.0, "hidden", (chunks - 1,))
    for k in range(chunks):
        far = k - n_near
        t = 18.0 + k * 0.4 if far < 0 else 29.0 + 0.5 * far
        t += 8.0 + 4.0 * (k if far < 0 else far)
        add(t, "middle", k)
        add(t + 6.0, "ready", k)
        add(t + 12.0, "spread", k)
        add(t + 17.0, "relay", k)
        add(max(t + 22.0, 60.0), "product", k)


def call_kernel(n_near, n_far, name, *args):
    smem = pl.BlockSpec(memory_space=pltpu.SMEM)
    hbm = pl.BlockSpec(memory_space=pl.ANY)
    n = n_near + n_far
    i16, f32, bf16 = jnp.int16, jnp.float32, jnp.bfloat16
    copies = 13 * n + 11 + 22 + 3 + 10
    return pl.pallas_call(
        functools.partial(kernel, n_near, n_far),
        out_shape=jax.ShapeDtypeStruct((3, 16), f32),
        in_specs=[smem] * 4 + [hbm] * 4,
        out_specs=pl.BlockSpec(memory_space=pltpu.VMEM),
        scratch_shapes=[
            pltpu.VMEM((ROWS, 1792), bf16),
            pltpu.VMEM((ROWS, 512), bf16),
            pltpu.VMEM((1024, 1792), bf16),
            pltpu.VMEM((1024, 512), bf16),
            pltpu.VMEM((n, ROWS, 128), f32),
            pltpu.VMEM((n, ROWS, 128), f32),
            pltpu.VMEM((n, 128, 1024), bf16),
            pltpu.VMEM((512, 128 * n_far), bf16),
            pltpu.VMEM((1792, 128 * n_far), bf16),
            pltpu.VMEM((n, 3, QUARTER + CODE, 128), i16),
            pltpu.VMEM((n, 3, QUARTER + CODE, 128), i16),
            pltpu.VMEM((n, 3, SLOT, 128), i16),
            pltpu.VMEM((n, 3, SLOT, 128), i16),
            pltpu.VMEM((n, 4, SLOT, 128), i16),
            pltpu.VMEM((n, 4 * BLOCK, 128), i16),
            pltpu.VMEM((2, 8, 128), f32),
            pltpu.VMEM((8, 8, 128), f32),
            pltpu.VMEM((8, 8, 128), f32),
            pltpu.VMEM((4, 8, 128), f32),
            pltpu.SemaphoreType.DMA((copies,)),
            pltpu.SemaphoreType.DMA((copies,)),
            pltpu.SemaphoreType.DMA((4,)),
        ],
        compiler_params=pltpu.CompilerParams(
            collective_id=n, has_side_effects=True, vmem_limit_bytes=56 * 2**20
        ),
        name=name,
    )(*args)


VARIANTS = ((4, 4), (2, 4), (2, 3))


def local(
    train_hidden,
    train_grad,
    val_hidden,
    val_grad,
    train_lengths,
    train_buckets,
    val_lengths,
    bucket_weight,
):
    args = (
        train_lengths,
        train_buckets,
        val_lengths,
        bucket_weight,
        train_hidden.reshape(HALF, 1792),
        train_grad.reshape(HALF, 512),
        val_hidden.reshape(128, 1792),
        val_grad.reshape(128, 512),
    )
    near = jnp.sum(val_lengths.reshape(2, 4, 2), axis=1)
    every = jnp.sum(near, axis=0, keepdims=True)
    fits = [
        jnp.all(every - jnp.minimum(near, 128 * a) <= 128 * b).astype(jnp.int32)
        for a, b in VARIANTS[1:]
    ]
    return lax.switch(
        sum(fits),
        [functools.partial(call_kernel, a, b, "ghost%d" % (a + b)) for a, b in VARIANTS],
        *args,
    )


def solution(mesh):
    placed = (
        P("dp", None, "tensor"),
        P("dp", None, "tensor"),
        P("dp", None, "tensor"),
        P("dp", None, "tensor"),
        P("dp"),
        P("dp"),
        P(),
        P(),
    )
    return jax.shard_map(
        local, mesh=mesh, in_specs=placed, out_specs=P("dp", None), check_vma=False
    )
```

```python
import functools
import math

import jax
import jax.numpy as jnp
from jax import lax
from jax.experimental import pallas as pl
from jax.experimental.pallas import tpu as pltpu
from jax.sharding import PartitionSpec as P

MESH = pl.DeviceIdType.MESH
D = 8192
FF = 28672
TOP = 32000.0
STEPS = 8.0
ROWS = 1536
HALF = 768
PIECE = 96
CODE = 16
SLOT = PIECE + CODE
QUARTER = 384
BLOCK = QUARTER + CODE
UP = 192
TILE_G = 512
TILE_H = 512
IN_TURN = 48


def quantize(x):
    top = jnp.maximum(jnp.max(jnp.abs(x), axis=0, keepdims=True), 1e-30)
    code = jnp.ceil(jnp.log2(top) * STEPS)
    q = jnp.round(x * (jnp.exp2(code * (-1.0 / STEPS)) * TOP)).astype(jnp.int32).astype(jnp.int16)
    return q, jnp.broadcast_to(code, (CODE, x.shape[1])).astype(jnp.int32).astype(jnp.int16)


def step_of(code, rows=1):
    code = code.astype(jnp.int32).astype(jnp.float32)
    return jnp.exp2(code[:rows] * (1.0 / STEPS)) * (1.0 / TOP)


def widen(q):
    return q.astype(jnp.int32).astype(jnp.float32)


def kernel(
    n_near,
    n_far,
    tl,
    tb,
    vl,
    bw,
    th,
    tg,
    vh,
    vg,
    out,
    th_b,
    tg_b,
    vh_b,
    vg_b,
    gram,
    hid,
    pick,
    right_g,
    right_h,
    sy,
    ry,
    sz,
    rz,
    az,
    g_all,
    info,
    total,
    fin1,
    fin2,
    ssem,
    rsem,
    lsem,
):
    chunks = n_near + n_far
    dp, tn = lax.axis_index("dp"), lax.axis_index("tensor")
    zh, x, c = dp // 8, (dp // 2) % 4, dp % 2
    zl, y = tn // 4, tn % 4

    def dev(zh=zh, x=x, c=c, zl=zl, y=y):
        return (zh * 8 + x * 2 + c, zl * 4 + y)

    sib = dev(c=1 - c)
    zhp = dev(zh=1 - zh)
    xp, xm, x2 = dev(x=(x + 1) % 4), dev(x=(x + 3) % 4), dev(x=(x + 2) % 4)
    zhp2, xp2, xm2, x22 = (
        (zhp, dev(zh=1 - zh, c=1 - c)),
        (xp, dev(x=(x + 1) % 4, c=1 - c)),
        (xm, dev(x=(x + 3) % 4, c=1 - c)),
        (x2, dev(x=(x + 2) % 4, c=1 - c)),
    )
    ys = [dev(y=(y + i) % 4) for i in (1, 2, 3)]
    zs = [dev(zl=(zl + i) % 4) for i in (1, 2, 3)]
    fin_y = [
        dev(c=(c + dc) % 2, y=(y + dy) % 4) for dc in range(2) for dy in range(4) if dc + dy > 0
    ]

    pending = []
    count = [0]

    def send(src, dst, to):
        i = count[0]
        count[0] += 1
        if i >= IN_TURN:
            pending[i - IN_TURN].wait_send()
        copy = pltpu.make_async_remote_copy(
            src_ref=src,
            dst_ref=dst,
            send_sem=ssem.at[i % IN_TURN],
            recv_sem=rsem.at[i],
            device_id=to,
            device_id_type=MESH,
        )
        copy.start()
        pending.append(copy)
        return copy

    own = [
        pltpu.make_async_copy(vg.at[:, 0], vg_b.at[0, 0], lsem.at[0]),
        pltpu.make_async_copy(tg, tg_b.at[pl.ds(0, HALF)], lsem.at[1]),
        pltpu.make_async_copy(vh.at[:, 0], vh_b.at[0, 0], lsem.at[2]),
        pltpu.make_async_copy(th, th_b.at[pl.ds(0, HALF)], lsem.at[3]),
    ]
    for copy in own:
        copy.start()
    row8 = lax.broadcasted_iota(jnp.int32, (8, 128), 0)
    lane8 = lax.broadcasted_iota(jnp.int32, (8, 128), 1)
    info[0] = jnp.where(row8 == 0, tl[0], jnp.where(row8 == 1, tl[1], tl[2])).astype(jnp.float32)

    barrier = pltpu.get_barrier_semaphore()
    peers = [*zhp2, *xp2, *xm2, *x22] + zs + fin_y
    for peer in peers:
        pl.semaphore_signal(barrier, inc=1, device_id=peer, device_id_type=MESH)
    pl.semaphore_wait(barrier, len(peers))

    arrived = {}
    for e in range(2):
        arrived["g", 4, e] = send(vg.at[:, e], vg_b.at[4, e], zhp2[e])
    for e in range(2):
        arrived["g", 1, e] = send(vg.at[:, e], vg_b.at[1, e], xp2[e])
        arrived["g", 2, e] = send(vg.at[:, e], vg_b.at[2, e], xm2[e])
        arrived["g", 3, e] = send(vg.at[:, e], vg_b.at[3, e], x22[e])
    arrived["g", 0, 1] = send(vg.at[:, 1], vg_b.at[0, 1], sib)
    arrived["tg"] = send(tg, tg_b.at[pl.ds(HALF, HALF)], sib)
    arrived["info"] = send(info.at[0], info.at[1], sib)

    prompts, lens, begins = [], [], []
    near = 0
    so_far = 0
    for s in range(8):
        r = (0, 1, 3, 2)[s % 4]
        chip = ((zh + s // 4) % 2) * 8 + ((x + 4 - r) % 4) * 2
        for e in range(2):
            prompt = chip + (c + e) % 2
            tokens = vl[prompt]
            held = 0
            for group in range(4):
                held = held + jnp.clip(tokens - 32 * group - 16 * e, 0, 16)
            prompts.append(prompt)
            lens.append(held)
            begins.append(so_far)
            so_far = so_far + held
        if s == 3:
            near = so_far
    near_done = jnp.minimum(near, 128 * n_near)
    everything = so_far

    def chunk_range(k):
        if k < n_near:
            return 128 * k, 0, 4
        return everything - 128 * (chunks - k), near_done, 8

    def fill_pick(k):
        start, least, places = chunk_range(k)
        row = lax.broadcasted_iota(jnp.int32, (128, 128), 0)
        col = lax.broadcasted_iota(jnp.int32, (128, 128), 1)
        for s in range(places):
            first = col < 64
            rank = col + jnp.where(first, begins[2 * s], begins[2 * s + 1] - 64)
            end = jnp.where(first, lens[2 * s], lens[2 * s + 1] + 64)
            hit = (rank - start == row) & (col < end) & (rank >= least)
            pick[k, :, pl.ds(128 * s, 128)] = jnp.where(hit, 1.0, 0.0).astype(jnp.bfloat16)

    def packed(k, ref, places):
        return lax.dot_general(
            pick[k, :, pl.ds(0, 128 * places)],
            ref[pl.ds(0, places)].reshape(128 * places, ref.shape[-1]),
            (((1,), (0,)), ((), ())),
            preferred_element_type=jnp.float32,
        )

    ops = []

    def at(time, fn):
        ops.append((time, len(ops), fn))

    def part(q):
        return q // 2, pl.ds(q % 2 * 2, 2)

    def start_far():
        for q in range(4):
            e, groups = part(q)
            arrived["h", 4, q] = send(vh.at[groups, e], vh_b.at[4, e, groups], zhp2[e])

    def start_near(h):
        arrived["h", 1, h] = send(vh.at[:, h], vh_b.at[1, h], xp2[h])
        arrived["h", 2, 1 - h] = send(vh.at[:, 1 - h], vh_b.at[2, 1 - h], xm2[1 - h])

    def start_train():
        arrived["th"] = send(th, th_b.at[pl.ds(HALF, HALF)], sib)
        arrived["h", 0, 1] = send(vh.at[:, 1], vh_b.at[0, 1], sib)

    waited = set()

    def have(key):
        if key not in waited:
            waited.add(key)
            arrived[key].wait_recv()

    def forward_near():
        have(("h", 1, 0))
        arrived["h", 3, 0] = send(vh_b.at[1, 0], vh_b.at[3, 0], xp)
        have(("h", 2, 1))
        arrived["h", 3, 1] = send(vh_b.at[2, 1], vh_b.at[3, 1], xm)

    def forward_far(q):
        have(("h", 4, q))
        e, groups = part(q)
        arrived["h", 5, q] = send(vh_b.at[4, e, groups], vh_b.at[5, e, groups], xp)
        arrived["h", 6, q] = send(vh_b.at[4, e, groups], vh_b.at[6, e, groups], xm)

    def forward_last(q):
        s, to = (5, xp) if q % 2 == 0 else (6, xm)
        have(("h", s, q))
        e, groups = part(q)
        arrived["h", 7, q] = send(vh_b.at[s, e, groups], vh_b.at[7, e, groups], to)

    def forward_grad(e):
        have(("g", 4, e))
        for s, to in ((5, xp), (6, xm), (7, x2)):
            arrived["g", s, e] = send(vg_b.at[4, e], vg_b.at[s, e], to)

    def mask_train():
        own[1].wait()
        have("info")
        have("tg")
        token = lax.broadcasted_iota(jnp.int32, (256, 128), 0).astype(jnp.float32)
        for i in range(6):
            keep = token < info[i // 3, i % 3 : i % 3 + 1, :]
            rows = pl.ds(256 * i, 256)
            for j in range(4):
                cols = pl.ds(128 * j, 128)
                tg_b[rows, cols] = jnp.where(
                    keep, tg_b[rows, cols].astype(jnp.float32), 0.0
                ).astype(jnp.bfloat16)

    def multiply(ks, left, ref, places, right, tile, to):
        for j, k in enumerate(ks):
            right[:, pl.ds(128 * j, 128)] = packed(k, ref, places).T.astype(jnp.bfloat16)

        @pl.loop(0, ROWS // tile)
        def _(i):
            rows = pl.ds(pl.multiple_of(i * tile, tile), tile)
            both = jnp.dot(
                left[rows, :],
                right[:, pl.ds(0, 128 * len(ks))],
                preferred_element_type=jnp.float32,
            )
            for j, k in enumerate(ks):
                to[k, rows, :] = both[:, 128 * j : 128 * j + 128]

    def put(ref, index, x):
        n = x.shape[0]
        q, code = quantize(x)
        ref[*index, pl.ds(0, n), :] = q
        ref[*index, pl.ds(n, CODE), :] = code

    def begin(ks):
        places = chunk_range(ks[0])[2]
        if 0 in ks:
            own[0].wait()
        have(("g", 0, 1))
        for s in range(1, places):
            have(("g", s, 0))
            have(("g", s, 1))
        for k in ks:
            fill_pick(k)
        multiply(ks, tg_b, vg_b, places, right_g, TILE_G, gram)
        for k in ks:
            for i in range(3):
                theirs = pl.multiple_of(((y + 1 + i) % 4) * QUARTER, QUARTER)
                put(sy, (k, i), gram[k, pl.ds(theirs, QUARTER), :])
                arrived["y", k, i] = send(sy.at[k, i], ry.at[k, i], ys[i])

    def middle(k):
        for i in range(3):
            have(("y", k, i))
        scales = [step_of(ry[k, i, pl.ds(QUARTER, CODE), :]) for i in range(3)]

        def summed(part):
            here = pl.ds(pl.multiple_of(part * PIECE, PIECE), PIECE)
            there = pl.ds(pl.multiple_of(y * QUARTER + part * PIECE, PIECE), PIECE)
            value = gram[k, there, :]
            for i in range(3):
                value = value + widen(ry[k, i, here, :]) * scales[i]
            return there, value

        for i in range(3):
            put(sz, (k, i), summed((zl + 1 + i) % 4)[1])
            arrived["z", k, i] = send(sz.at[k, i], rz.at[k, i], zs[i])
        there, value = summed(zl)
        gram[k, there, :] = value

    def ready(k):
        for i in range(3):
            have(("z", k, i))
        there = pl.ds(pl.multiple_of(y * QUARTER + zl * PIECE, PIECE), PIECE)
        value = gram[k, there, :]
        for i in range(3):
            scale = step_of(rz[k, i, pl.ds(PIECE, CODE), :])
            value = value + widen(rz[k, i, pl.ds(0, PIECE), :]) * scale
        put(az, (k, 0), value)
        for i in range(3):
            arrived["az", k, i] = send(az.at[k, 0], az.at[k, 1 + i], zs[i])

    def block(k, i, first=0, rows=BLOCK):
        owner = (y + i) % 4
        return g_all.at[k, pl.ds(pl.multiple_of(owner * BLOCK + first, CODE), rows)]

    def spread(k):
        for i in range(3):
            have(("az", k, i))
        codes = jnp.zeros((CODE, 128), jnp.int32)
        row = lax.broadcasted_iota(jnp.int32, (CODE, 128), 0)
        for i in range(4):
            part = (zl + 4 - i) % 4
            spot = pl.multiple_of(y * BLOCK + part * PIECE, CODE)
            g_all[k, pl.ds(spot, PIECE), :] = az[k, i, pl.ds(0, PIECE), :]
            code = az[k, i, pl.ds(PIECE, CODE), :].astype(jnp.int32)
            codes = jnp.where(row == part, code, codes)
        g_all[k, pl.ds(pl.multiple_of(y * BLOCK + QUARTER, CODE), CODE), :] = codes.astype(jnp.int16)
        arrived["up", k] = send(block(k, 0), block(k, 0), ys[0])
        arrived["down", k] = send(block(k, 0), block(k, 0), ys[2])

    def relay(k):
        have(("up", k))
        rows = block(k, 3, 0, UP)
        arrived["up2", k] = send(rows, rows, ys[0])
        have(("down", k))
        rows = block(k, 1, UP, BLOCK - UP)
        arrived["down2", k] = send(rows, rows, ys[2])

    def hidden(ks):
        near_only, last = ks[-1] < n_near, ks[-1] == chunks - 1
        places = 4 if near_only else 8 if last else 7
        if 0 in ks:
            own[2].wait()
            own[3].wait()
            have("th")
        have(("h", 0, 1))
        for s in range(1, places):
            for i in range(2 if s < 4 else 4):
                have(("h", s, i))
        multiply(ks, th_b, vh_b, places, right_h, TILE_H, hid)

    total[...] = jnp.zeros_like(total)

    def product(k):
        have(("up2", k))
        have(("down2", k))
        sums = [None] * 6
        for p in range(16):
            top = p // 4 * BLOCK
            if p % 4 == 0:
                steps = step_of(g_all[k, pl.ds(top + QUARTER, CODE), :], 8)
            scale = steps[p % 4 : p % 4 + 1]
            here = pl.ds(top + p % 4 * PIECE, PIECE)
            both = hid[k, pl.ds(p * PIECE, PIECE), :] * widen(g_all[k, here, :])
            parts = {}
            for u in range(6):
                i = (p * 6 + u) // 16
                part = both[16 * u : 16 * u + 8] + both[16 * u + 8 : 16 * u + 16]
                parts[i] = part if i not in parts else parts[i] + part
            for i, part in parts.items():
                part = part * scale
                sums[i] = part if sums[i] is None else sums[i] + part
        tile = jnp.zeros((8, 128), jnp.float32)
        for i in range(6):
            tile = jnp.where(row8 == i, jnp.sum(sums[i], axis=0, keepdims=True), tile)
        start, least, places = chunk_range(k)
        rank = lane8 + start
        for s in range(2 * places):
            mine = (rank >= begins[s]) & (rank < begins[s] + lens[s]) & (rank >= least)
            total[s] += jnp.where(mine, tile, 0.0)

    do = dict(
        start_far=start_far,
        start_near=start_near,
        start_train=start_train,
        forward_near=forward_near,
        forward_far=forward_far,
        forward_last=forward_last,
        forward_grad=forward_grad,
        mask_train=mask_train,
        begin=begin,
        middle=middle,
        ready=ready,
        spread=spread,
        relay=relay,
        hidden=hidden,
        product=product,
    )
    plan(chunks, n_near, at, do)
    for _, _, fn in sorted(ops, key=lambda op: op[:2]):
        fn()

    mine = jnp.zeros((8, 128), jnp.float32)
    for s in range(16):
        mine = jnp.where(lane8 == prompts[s], jnp.sum(total[s], axis=1, keepdims=True), mine)
    turned = jnp.where(row8 < 3, pltpu.roll(mine, 5, 0), pltpu.roll(mine, 3, 0))
    fin1[0] = jnp.where(c == 0, mine, turned)
    last = [send(fin1.at[0], fin1.at[1 + i], peer) for i, peer in enumerate(fin_y)]
    for copy in last:
        copy.wait_recv()
    fin2[0] = jnp.sum(fin1[...], axis=0)
    last = [send(fin2.at[0], fin2.at[1 + i], peer) for i, peer in enumerate(zs)]
    for copy in last:
        copy.wait_recv()
    pair = jnp.sum(fin2[...], axis=0)
    pair = jnp.where(c == 0, pair, pltpu.roll(pair, 5, 0))
    weight = jnp.where(row8 == 0, bw[tb[0]], jnp.where(row8 == 1, bw[tb[1]], bw[tb[2]]))
    val_counts = jnp.ones((8, 128), jnp.float32)
    for j in range(16):
        val_counts = jnp.where(lane8 == j, vl[j].astype(jnp.float32), val_counts)
    scores = pair * weight / (math.sqrt(FF * D) * jnp.sqrt(info[0] * val_counts))
    out[...] = scores[:3, :16]
    for copy in pending[-IN_TURN:]:
        copy.wait_send()


def plan(chunks, n_near, at, do):
    def add(time, name, *args):
        at(time, functools.partial(do[name], *args))

    add(15.5, "start_far")
    add(0.1, "start_train")
    add(15.6, "start_near", 0)
    add(16.0, "mask_train")
    add(19.0, "forward_grad", 0)
    add(21.0, "forward_grad", 1)
    add(21.1, "start_near", 1)
    add(29.5, "forward_near")
    for q in range(4):
        add([35.5, 39.0, 44.0, 48.0][q], "forward_far", q)
        add([41.0, 45.0, 49.0, 53.0][q], "forward_last", q)
    add(18.0, "begin", tuple(range(n_near)))
    add(27.0, "begin", tuple(range(n_near, chunks)))
    add(47.0, "hidden", tuple(range(n_near)))
    add(55.0, "hidden", tuple(range(n_near, chunks - 1)))
    add(58.5, "hidden", (chunks - 1,))
    for k in range(chunks):
        far = k - n_near
        near_times = [t + 0.5 * k for t in [30, 37, 43, 48, 65]]
        far_times = [t + 4.0 * far for t in [38.2, 44.5, 50, 55, 66.0]]
        names = ("middle", "ready", "spread", "relay", "product")
        for t, name in zip(near_times if far < 0 else far_times, names):
            add(t, name, k)


def call_kernel(n_near, n_far, name, *args):
    smem = pl.BlockSpec(memory_space=pltpu.SMEM)
    hbm = pl.BlockSpec(memory_space=pl.ANY)
    n = n_near + n_far
    i16, f32, bf16 = jnp.int16, jnp.float32, jnp.bfloat16
    copies = 13 * n + 51
    return pl.pallas_call(
        functools.partial(kernel, n_near, n_far),
        out_shape=jax.ShapeDtypeStruct((3, 16), f32),
        in_specs=[smem] * 4 + [hbm] * 4,
        out_specs=pl.BlockSpec(memory_space=pltpu.VMEM),
        scratch_shapes=[
            pltpu.VMEM((ROWS, 1792), bf16),
            pltpu.VMEM((ROWS, 512), bf16),
            pltpu.VMEM((8, 2, 4, 16, 1792), bf16),
            pltpu.VMEM((8, 2, 4, 16, 512), bf16),
            pltpu.VMEM((n, ROWS, 128), f32),
            pltpu.VMEM((n, ROWS, 128), f32),
            pltpu.VMEM((n, 128, 1024), bf16),
            pltpu.VMEM((512, 128 * n_far), bf16),
            pltpu.VMEM((1792, 128 * n_far), bf16),
            pltpu.VMEM((n, 3, QUARTER + CODE, 128), i16),
            pltpu.VMEM((n, 3, QUARTER + CODE, 128), i16),
            pltpu.VMEM((n, 3, SLOT, 128), i16),
            pltpu.VMEM((n, 3, SLOT, 128), i16),
            pltpu.VMEM((n, 4, SLOT, 128), i16),
            pltpu.VMEM((n, 4 * BLOCK, 128), i16),
            pltpu.VMEM((2, 8, 128), f32),
            pltpu.VMEM((16, 8, 128), f32),
            pltpu.VMEM((8, 8, 128), f32),
            pltpu.VMEM((4, 8, 128), f32),
            pltpu.SemaphoreType.DMA((IN_TURN,)),
            pltpu.SemaphoreType.DMA((copies,)),
            pltpu.SemaphoreType.DMA((4,)),
        ],
        compiler_params=pltpu.CompilerParams(
            collective_id=n, has_side_effects=True, vmem_limit_bytes=56 * 2**20
        ),
        name=name,
    )(*args)


VARIANTS = ((4, 4), (2, 3), (2, 2))


def local(
    train_hidden,
    train_grad,
    val_hidden,
    val_grad,
    train_lengths,
    train_buckets,
    val_lengths,
    bucket_weight,
):
    args = (
        train_lengths,
        train_buckets,
        val_lengths,
        bucket_weight,
        train_hidden.reshape(HALF, 1792),
        train_grad.reshape(HALF, 512),
        val_hidden.reshape(4, 2, 16, 1792),
        val_grad.reshape(4, 2, 16, 512),
    )
    prompt = jnp.arange(16)[None, :]
    row = jnp.arange(4)[:, None]
    stay = sum(jnp.clip(val_lengths - 32 * group, 0, 16) for group in range(4))[None, :]
    held = jnp.where(prompt % 2 == row % 2, stay, val_lengths[None, :] - stay)
    near = jnp.sum(jnp.where(prompt // 8 == row // 2, held, 0), axis=1)
    every = jnp.sum(held, axis=1)
    fits = [
        jnp.all(every - jnp.minimum(near, 128 * a) <= 128 * b).astype(jnp.int32)
        for a, b in VARIANTS[1:]
    ]
    return lax.switch(
        sum(fits),
        [functools.partial(call_kernel, a, b, "ghost%d" % (a + b)) for a, b in VARIANTS],
        *args,
    )


def solution(mesh):
    placed = (
        P("dp", None, "tensor"),
        P("dp", None, "tensor"),
        P("dp", None, "tensor"),
        P("dp", None, "tensor"),
        P("dp"),
        P("dp"),
        P(),
        P(),
    )
    return jax.shard_map(
        local, mesh=mesh, in_specs=placed, out_specs=P("dp", None), check_vma=False
    )
```

```python
import functools
import math

import jax
import jax.numpy as jnp
from jax import lax
from jax.experimental import pallas as pl
from jax.experimental.pallas import tpu as pltpu
from jax.sharding import PartitionSpec as P

MESH = pl.DeviceIdType.MESH
D = 8192
FF = 28672
TOP = 32000.0
STEPS = 8.0
ROWS = 1536
HALF = 768
PIECE = 96
CODE = 16
SLOT = PIECE + CODE
QUARTER = 384
BLOCK = QUARTER + CODE
UP = 192
TILE_G = 512
TILE_H = 512
IN_TURN = 48


def quantize(x):
    top = jnp.maximum(jnp.max(jnp.abs(x), axis=0, keepdims=True), 1e-30)
    code = jnp.ceil(jnp.log2(top) * STEPS)
    q = jnp.round(x * (jnp.exp2(code * (-1.0 / STEPS)) * TOP)).astype(jnp.int32).astype(jnp.int16)
    return q, jnp.broadcast_to(code, (CODE, x.shape[1])).astype(jnp.int32).astype(jnp.int16)


def step_of(code, rows=1):
    code = code.astype(jnp.int32).astype(jnp.float32)
    return jnp.exp2(code[:rows] * (1.0 / STEPS)) * (1.0 / TOP)


def widen(q):
    return q.astype(jnp.int32).astype(jnp.float32)


def kernel(
    n_near,
    n_far,
    tl,
    tb,
    vl,
    bw,
    th,
    tg,
    vh,
    vg,
    out,
    th_b,
    tg_b,
    vh_b,
    vg_b,
    gram,
    hid,
    pick,
    right_g,
    right_h,
    sy,
    ry,
    sz,
    rz,
    az,
    g_all,
    info,
    total,
    fin1,
    fin2,
    ssem,
    rsem,
    lsem,
):
    chunks = n_near + n_far
    dp, tn = lax.axis_index("dp"), lax.axis_index("tensor")
    zh, x, c = dp // 8, (dp // 2) % 4, dp % 2
    zl, y = tn // 4, tn % 4

    def dev(zh=zh, x=x, c=c, zl=zl, y=y):
        return (zh * 8 + x * 2 + c, zl * 4 + y)

    sib = dev(c=1 - c)
    zhp = dev(zh=1 - zh)
    xp, xm, x2 = dev(x=(x + 1) % 4), dev(x=(x + 3) % 4), dev(x=(x + 2) % 4)
    zhp2, xp2, xm2, x22 = (
        (zhp, dev(zh=1 - zh, c=1 - c)),
        (xp, dev(x=(x + 1) % 4, c=1 - c)),
        (xm, dev(x=(x + 3) % 4, c=1 - c)),
        (x2, dev(x=(x + 2) % 4, c=1 - c)),
    )
    ys = [dev(y=(y + i) % 4) for i in (1, 2, 3)]
    zs = [dev(zl=(zl + i) % 4) for i in (1, 2, 3)]
    fin_y = [
        dev(c=(c + dc) % 2, y=(y + dy) % 4) for dc in range(2) for dy in range(4) if dc + dy > 0
    ]

    pending = []
    count = [0]

    def send(src, dst, to):
        i = count[0]
        count[0] += 1
        if i >= IN_TURN:
            pending[i - IN_TURN].wait_send()
        copy = pltpu.make_async_remote_copy(
            src_ref=src,
            dst_ref=dst,
            send_sem=ssem.at[i % IN_TURN],
            recv_sem=rsem.at[i],
            device_id=to,
            device_id_type=MESH,
        )
        copy.start()
        pending.append(copy)
        return copy

    own = [
        pltpu.make_async_copy(vg.at[:, 0], vg_b.at[0, 0], lsem.at[0]),
        pltpu.make_async_copy(tg, tg_b.at[pl.ds(0, HALF)], lsem.at[1]),
        pltpu.make_async_copy(vh.at[:, 0], vh_b.at[0, 0], lsem.at[2]),
        pltpu.make_async_copy(th, th_b.at[pl.ds(0, HALF)], lsem.at[3]),
    ]
    for copy in own:
        copy.start()
    row8 = lax.broadcasted_iota(jnp.int32, (8, 128), 0)
    lane8 = lax.broadcasted_iota(jnp.int32, (8, 128), 1)
    info[0] = jnp.where(row8 == 0, tl[0], jnp.where(row8 == 1, tl[1], tl[2])).astype(jnp.float32)

    barrier = pltpu.get_barrier_semaphore()
    peers = [*zhp2, *xp2, *xm2, *x22] + zs + fin_y
    for peer in peers:
        pl.semaphore_signal(barrier, inc=1, device_id=peer, device_id_type=MESH)
    pl.semaphore_wait(barrier, len(peers))

    arrived = {}
    for e in range(2):
        arrived["g", 4, e] = send(vg.at[:, e], vg_b.at[4, e], zhp2[e])
    for e in range(2):
        arrived["g", 1, e] = send(vg.at[:, e], vg_b.at[1, e], xp2[e])
        arrived["g", 2, e] = send(vg.at[:, e], vg_b.at[2, e], xm2[e])
        arrived["g", 3, e] = send(vg.at[:, e], vg_b.at[3, e], x22[e])
    arrived["g", 0, 1] = send(vg.at[:, 1], vg_b.at[0, 1], sib)
    arrived["tg"] = send(tg, tg_b.at[pl.ds(HALF, HALF)], sib)
    arrived["info"] = send(info.at[0], info.at[1], sib)

    prompts, lens, begins = [], [], []
    near = 0
    so_far = 0
    for s in range(8):
        r = (0, 1, 3, 2)[s % 4]
        chip = ((zh + s // 4) % 2) * 8 + ((x + 4 - r) % 4) * 2
        for e in range(2):
            prompt = chip + (c + e) % 2
            tokens = vl[prompt]
            held = 0
            for group in range(4):
                held = held + jnp.clip(tokens - 32 * group - 16 * e, 0, 16)
            prompts.append(prompt)
            lens.append(held)
            begins.append(so_far)
            so_far = so_far + held
        if s == 3:
            near = so_far
    near_done = jnp.minimum(near, 128 * n_near)
    everything = so_far

    def chunk_range(k):
        if k < n_near:
            return 128 * k, 0, 4
        return everything - 128 * (chunks - k), near_done, 8

    def fill_pick(k):
        start, least, places = chunk_range(k)
        row = lax.broadcasted_iota(jnp.int32, (128, 128), 0)
        col = lax.broadcasted_iota(jnp.int32, (128, 128), 1)
        for s in range(places):
            first = col < 64
            rank = col + jnp.where(first, begins[2 * s], begins[2 * s + 1] - 64)
            end = jnp.where(first, lens[2 * s], lens[2 * s + 1] + 64)
            hit = (rank - start == row) & (col < end) & (rank >= least)
            pick[k, :, pl.ds(128 * s, 128)] = jnp.where(hit, 1.0, 0.0).astype(jnp.bfloat16)

    def packed(k, ref, places):
        return lax.dot_general(
            pick[k, :, pl.ds(0, 128 * places)],
            ref[pl.ds(0, places)].reshape(128 * places, ref.shape[-1]),
            (((1,), (0,)), ((), ())),
            preferred_element_type=jnp.float32,
        )

    ops = []

    def at(time, fn):
        ops.append((time, len(ops), fn))

    def part(q):
        return q // 2, pl.ds(q % 2 * 2, 2)

    def start_far():
        for q in range(4):
            e, groups = part(q)
            arrived["h", 4, q] = send(vh.at[groups, e], vh_b.at[4, e, groups], zhp2[e])

    def start_near(h):
        arrived["h", 1, h] = send(vh.at[:, h], vh_b.at[1, h], xp2[h])
        arrived["h", 2, 1 - h] = send(vh.at[:, 1 - h], vh_b.at[2, 1 - h], xm2[1 - h])

    def start_train():
        arrived["th"] = send(th, th_b.at[pl.ds(HALF, HALF)], sib)
        arrived["h", 0, 1] = send(vh.at[:, 1], vh_b.at[0, 1], sib)

    waited = set()

    def have(key):
        if key not in waited:
            waited.add(key)
            arrived[key].wait_recv()

    def forward_near():
        have(("h", 1, 0))
        arrived["h", 3, 0] = send(vh_b.at[1, 0], vh_b.at[3, 0], xp)
        have(("h", 2, 1))
        arrived["h", 3, 1] = send(vh_b.at[2, 1], vh_b.at[3, 1], xm)

    def forward_far(q):
        have(("h", 4, q))
        e, groups = part(q)
        arrived["h", 5, q] = send(vh_b.at[4, e, groups], vh_b.at[5, e, groups], xp)
        arrived["h", 6, q] = send(vh_b.at[4, e, groups], vh_b.at[6, e, groups], xm)

    def forward_last(q):
        s, to = (5, xp) if q % 2 == 0 else (6, xm)
        have(("h", s, q))
        e, groups = part(q)
        arrived["h", 7, q] = send(vh_b.at[s, e, groups], vh_b.at[7, e, groups], to)

    def forward_grad(e):
        have(("g", 4, e))
        for s, to in ((5, xp), (6, xm), (7, x2)):
            arrived["g", s, e] = send(vg_b.at[4, e], vg_b.at[s, e], to)

    def mask_train():
        own[1].wait()
        have("info")
        have("tg")
        token = lax.broadcasted_iota(jnp.int32, (256, 128), 0).astype(jnp.float32)
        for i in range(6):
            keep = token < info[i // 3, i % 3 : i % 3 + 1, :]
            rows = pl.ds(256 * i, 256)
            for j in range(4):
                cols = pl.ds(128 * j, 128)
                tg_b[rows, cols] = jnp.where(
                    keep, tg_b[rows, cols].astype(jnp.float32), 0.0
                ).astype(jnp.bfloat16)

    def multiply(ks, left, ref, places, right, tile, to):
        for j, k in enumerate(ks):
            right[:, pl.ds(128 * j, 128)] = packed(k, ref, places).T.astype(jnp.bfloat16)

        @pl.loop(0, ROWS // tile)
        def _(i):
            rows = pl.ds(pl.multiple_of(i * tile, tile), tile)
            both = jnp.dot(
                left[rows, :],
                right[:, pl.ds(0, 128 * len(ks))],
                preferred_element_type=jnp.float32,
            )
            for j, k in enumerate(ks):
                to[k, rows, :] = both[:, 128 * j : 128 * j + 128]

    def put(ref, index, x):
        n = x.shape[0]
        q, code = quantize(x)
        ref[*index, pl.ds(0, n), :] = q
        ref[*index, pl.ds(n, CODE), :] = code

    def begin(ks):
        places = chunk_range(ks[0])[2]
        if 0 in ks:
            own[0].wait()
        have(("g", 0, 1))
        for s in range(1, places):
            have(("g", s, 0))
            have(("g", s, 1))
        for k in ks:
            fill_pick(k)
        multiply(ks, tg_b, vg_b, places, right_g, TILE_G, gram)
        for k in ks:
            for i in range(3):
                theirs = pl.multiple_of(((y + 1 + i) % 4) * QUARTER, QUARTER)
                put(sy, (k, i), gram[k, pl.ds(theirs, QUARTER), :])
                arrived["y", k, i] = send(sy.at[k, i], ry.at[k, i], ys[i])

    def middle(k):
        for i in range(3):
            have(("y", k, i))
        scales = [step_of(ry[k, i, pl.ds(QUARTER, CODE), :]) for i in range(3)]

        def summed(part):
            here = pl.ds(pl.multiple_of(part * PIECE, PIECE), PIECE)
            there = pl.ds(pl.multiple_of(y * QUARTER + part * PIECE, PIECE), PIECE)
            value = gram[k, there, :]
            for i in range(3):
                value = value + widen(ry[k, i, here, :]) * scales[i]
            return there, value

        for i in range(3):
            put(sz, (k, i), summed((zl + 1 + i) % 4)[1])
            arrived["z", k, i] = send(sz.at[k, i], rz.at[k, i], zs[i])
        there, value = summed(zl)
        gram[k, there, :] = value

    def ready(k):
        for i in range(3):
            have(("z", k, i))
        there = pl.ds(pl.multiple_of(y * QUARTER + zl * PIECE, PIECE), PIECE)
        value = gram[k, there, :]
        for i in range(3):
            scale = step_of(rz[k, i, pl.ds(PIECE, CODE), :])
            value = value + widen(rz[k, i, pl.ds(0, PIECE), :]) * scale
        put(az, (k, 0), value)
        for i in range(3):
            arrived["az", k, i] = send(az.at[k, 0], az.at[k, 1 + i], zs[i])

    def block(k, i, first=0, rows=BLOCK):
        owner = (y + i) % 4
        return g_all.at[k, pl.ds(pl.multiple_of(owner * BLOCK + first, CODE), rows)]

    def spread(k):
        for i in range(3):
            have(("az", k, i))
        codes = jnp.zeros((CODE, 128), jnp.int32)
        row = lax.broadcasted_iota(jnp.int32, (CODE, 128), 0)
        for i in range(4):
            part = (zl + 4 - i) % 4
            spot = pl.multiple_of(y * BLOCK + part * PIECE, CODE)
            g_all[k, pl.ds(spot, PIECE), :] = az[k, i, pl.ds(0, PIECE), :]
            code = az[k, i, pl.ds(PIECE, CODE), :].astype(jnp.int32)
            codes = jnp.where(row == part, code, codes)
        g_all[k, pl.ds(pl.multiple_of(y * BLOCK + QUARTER, CODE), CODE), :] = codes.astype(jnp.int16)
        arrived["up", k] = send(block(k, 0), block(k, 0), ys[0])
        arrived["down", k] = send(block(k, 0), block(k, 0), ys[2])

    def relay(k):
        have(("up", k))
        rows = block(k, 3, 0, UP)
        arrived["up2", k] = send(rows, rows, ys[0])
        have(("down", k))
        rows = block(k, 1, UP, BLOCK - UP)
        arrived["down2", k] = send(rows, rows, ys[2])

    def hidden(ks):
        near_only, last = ks[-1] < n_near, ks[-1] == chunks - 1
        places = 4 if near_only else 8 if last else 7
        if 0 in ks:
            own[2].wait()
            own[3].wait()
            have("th")
        have(("h", 0, 1))
        for s in range(1, places):
            for i in range(2 if s < 4 else 4):
                have(("h", s, i))
        multiply(ks, th_b, vh_b, places, right_h, TILE_H, hid)

    total[...] = jnp.zeros_like(total)

    def product(k):
        have(("up2", k))
        have(("down2", k))
        sums = [None] * 6
        for p in range(16):
            top = p // 4 * BLOCK
            if p % 4 == 0:
                steps = step_of(g_all[k, pl.ds(top + QUARTER, CODE), :], 8)
            scale = steps[p % 4 : p % 4 + 1]
            here = pl.ds(top + p % 4 * PIECE, PIECE)
            both = hid[k, pl.ds(p * PIECE, PIECE), :] * widen(g_all[k, here, :])
            parts = {}
            for u in range(6):
                i = (p * 6 + u) // 16
                part = both[16 * u : 16 * u + 8] + both[16 * u + 8 : 16 * u + 16]
                parts[i] = part if i not in parts else parts[i] + part
            for i, part in parts.items():
                part = part * scale
                sums[i] = part if sums[i] is None else sums[i] + part
        tile = jnp.zeros((8, 128), jnp.float32)
        for i in range(6):
            tile = jnp.where(row8 == i, jnp.sum(sums[i], axis=0, keepdims=True), tile)
        start, least, places = chunk_range(k)
        rank = lane8 + start
        for s in range(2 * places):
            mine = (rank >= begins[s]) & (rank < begins[s] + lens[s]) & (rank >= least)
            total[s] += jnp.where(mine, tile, 0.0)

    do = dict(
        start_far=start_far,
        start_near=start_near,
        start_train=start_train,
        forward_near=forward_near,
        forward_far=forward_far,
        forward_last=forward_last,
        forward_grad=forward_grad,
        mask_train=mask_train,
        begin=begin,
        middle=middle,
        ready=ready,
        spread=spread,
        relay=relay,
        hidden=hidden,
        product=product,
    )
    plan(chunks, n_near, at, do)
    for _, _, fn in sorted(ops, key=lambda op: op[:2]):
        fn()

    mine = jnp.zeros((8, 128), jnp.float32)
    for s in range(16):
        mine = jnp.where(lane8 == prompts[s], jnp.sum(total[s], axis=1, keepdims=True), mine)
    turned = jnp.where(row8 < 3, pltpu.roll(mine, 5, 0), pltpu.roll(mine, 3, 0))
    fin1[0] = jnp.where(c == 0, mine, turned)
    last = [send(fin1.at[0], fin1.at[1 + i], peer) for i, peer in enumerate(fin_y)]
    for copy in last:
        copy.wait_recv()
    fin2[0] = jnp.sum(fin1[...], axis=0)
    last = [send(fin2.at[0], fin2.at[1 + i], peer) for i, peer in enumerate(zs)]
    for copy in last:
        copy.wait_recv()
    pair = jnp.sum(fin2[...], axis=0)
    pair = jnp.where(c == 0, pair, pltpu.roll(pair, 5, 0))
    weight = jnp.where(row8 == 0, bw[tb[0]], jnp.where(row8 == 1, bw[tb[1]], bw[tb[2]]))
    val_counts = jnp.ones((8, 128), jnp.float32)
    for j in range(16):
        val_counts = jnp.where(lane8 == j, vl[j].astype(jnp.float32), val_counts)
    scores = pair * weight / (math.sqrt(FF * D) * jnp.sqrt(info[0] * val_counts))
    out[...] = scores[:3, :16]
    for copy in pending[-IN_TURN:]:
        copy.wait_send()


def plan(chunks, n_near, at, do):
    def add(time, name, *args):
        at(time, functools.partial(do[name], *args))

    add(15.5, "start_far")
    add(0.1, "start_train")
    add(15.6, "start_near", 0)
    add(16.0, "mask_train")
    add(19.0, "forward_grad", 0)
    add(21.0, "forward_grad", 1)
    add(21.1, "start_near", 1)
    add(29.5, "forward_near")
    for q in range(4):
        add([35.5, 39.0, 44.0, 48.0][q], "forward_far", q)
        add([41.0, 45.0, 49.0, 53.0][q], "forward_last", q)
    add(18.0, "begin", tuple(range(n_near)))
    add(27.0, "begin", tuple(range(n_near, chunks)))
    add(47.0, "hidden", tuple(range(n_near)))
    add(55.0, "hidden", tuple(range(n_near, chunks - 1)))
    add(58.5, "hidden", (chunks - 1,))
    for k in range(chunks):
        far = k - n_near
        near_times = [t + 0.5 * k for t in [30, 37, 43, 48, 65]]
        far_times = [t + 4.0 * far for t in [38.2, 44.5, 50, 55, 66.0]]
        names = ("middle", "ready", "spread", "relay", "product")
        for t, name in zip(near_times if far < 0 else far_times, names):
            add(t, name, k)


def call_kernel(n_near, n_far, name, *args):
    smem = pl.BlockSpec(memory_space=pltpu.SMEM)
    hbm = pl.BlockSpec(memory_space=pl.ANY)
    n = n_near + n_far
    i16, f32, bf16 = jnp.int16, jnp.float32, jnp.bfloat16
    copies = 13 * n + 51
    return pl.pallas_call(
        functools.partial(kernel, n_near, n_far),
        out_shape=jax.ShapeDtypeStruct((3, 16), f32),
        in_specs=[smem] * 4 + [hbm] * 4,
        out_specs=pl.BlockSpec(memory_space=pltpu.VMEM),
        scratch_shapes=[
            pltpu.VMEM((ROWS, 1792), bf16),
            pltpu.VMEM((ROWS, 512), bf16),
            pltpu.VMEM((8, 2, 4, 16, 1792), bf16),
            pltpu.VMEM((8, 2, 4, 16, 512), bf16),
            pltpu.VMEM((n, ROWS, 128), f32),
            pltpu.VMEM((n, ROWS, 128), f32),
            pltpu.VMEM((n, 128, 1024), bf16),
            pltpu.VMEM((512, 128 * n_far), bf16),
            pltpu.VMEM((1792, 128 * n_far), bf16),
            pltpu.VMEM((n, 3, QUARTER + CODE, 128), i16),
            pltpu.VMEM((n, 3, QUARTER + CODE, 128), i16),
            pltpu.VMEM((n, 3, SLOT, 128), i16),
            pltpu.VMEM((n, 3, SLOT, 128), i16),
            pltpu.VMEM((n, 4, SLOT, 128), i16),
            pltpu.VMEM((n, 4 * BLOCK, 128), i16),
            pltpu.VMEM((2, 8, 128), f32),
            pltpu.VMEM((16, 8, 128), f32),
            pltpu.VMEM((8, 8, 128), f32),
            pltpu.VMEM((4, 8, 128), f32),
            pltpu.SemaphoreType.DMA((IN_TURN,)),
            pltpu.SemaphoreType.DMA((copies,)),
            pltpu.SemaphoreType.DMA((4,)),
        ],
        compiler_params=pltpu.CompilerParams(
            collective_id=n, has_side_effects=True, vmem_limit_bytes=56 * 2**20
        ),
        name=name,
    )(*args)


VARIANTS = ((4, 4), (2, 4), (2, 3))


def local(
    train_hidden,
    train_grad,
    val_hidden,
    val_grad,
    train_lengths,
    train_buckets,
    val_lengths,
    bucket_weight,
):
    args = (
        train_lengths,
        train_buckets,
        val_lengths,
        bucket_weight,
        train_hidden.reshape(HALF, 1792),
        train_grad.reshape(HALF, 512),
        val_hidden.reshape(4, 2, 16, 1792),
        val_grad.reshape(4, 2, 16, 512),
    )
    prompt = jnp.arange(16)[None, :]
    row = jnp.arange(4)[:, None]
    stay = sum(jnp.clip(val_lengths - 32 * group, 0, 16) for group in range(4))[None, :]
    held = jnp.where(prompt % 2 == row % 2, stay, val_lengths[None, :] - stay)
    near = jnp.sum(jnp.where(prompt // 8 == row // 2, held, 0), axis=1)
    every = jnp.sum(held, axis=1)
    fits = [
        jnp.all(every - jnp.minimum(near, 128 * a) <= 128 * b).astype(jnp.int32)
        for a, b in VARIANTS[1:]
    ]
    return lax.switch(
        sum(fits),
        [functools.partial(call_kernel, a, b, "ghost%d" % (a + b)) for a, b in VARIANTS],
        *args,
    )


def solution(mesh):
    placed = (
        P("dp", None, "tensor"),
        P("dp", None, "tensor"),
        P("dp", None, "tensor"),
        P("dp", None, "tensor"),
        P("dp"),
        P("dp"),
        P(),
        P(),
    )
    return jax.shard_map(
        local, mesh=mesh, in_specs=placed, out_specs=P("dp", None), check_vma=False
    )
```
